512 devices in a mesh: row: 16 (over y_hi, x, core), col: 32 (over z, y_lo).
Axes of the slice: x: 4, y: 4 (y_hi: 2, y_lo: 2; y = y_hi * 2 + y_lo), z: 16, core: 2. Of those that a mesh axis runs over, the one named last changes fastest.
Arguments:
- weight: bfloat16 [8192, 16384], P('row', 'col'), may hold values from -6 to 6
- gradient: bfloat16 [8192, 16384], P('row', 'col'), may hold values from -6 to 6
- old_basis: bfloat16 [8192, 1024], P('row'), may hold values from -0.0625 to 0.0625
- new_basis: bfloat16 [8192, 1024], P('row'), may hold values from -0.0625 to 0.0625
- first_moment: float32 [1024, 16384], P(None, ('col', 'row')), may hold values from -6 to 6
- second_moment: float32 [1024, 16384], P(None, ('col', 'row')), may hold values from 0.05 to 2
Outputs:
- new_weight: bfloat16 [8192, 16384], P('row', 'col')
- update: bfloat16 [8192, 16384], P('row', 'col')
- first_new: float32 [1024, 16384], P(None, ('col', 'row'))
- second_new: float32 [1024, 16384], P(None, ('col', 'row'))
The draws below stay inside these ranges and needn't reach their ends.
All inputs are finite; a program needn't handle non-finite values.
Results may differ from the reference program's by a relative error of at most 0.0047.
Values may be sent and summed in bfloat16 or wider, within the bound.
No kernel may reach another device: no remote copies, remote signals or barrier semaphores. Data moves between devices by JAX's collectives and lax.ppermute only.
A program may use at most 64 MiB of HBM per device.

```python
import math
import jax
import jax.numpy as jnp
from jax import lax

D = 8192
FF = 16384
RANK = 1024


def levels(stream_key, dims, shards, low, largest):
    loudness, own = 1.0, jax.random.fold_in(stream_key, 6)
    for position, shards_of in shards:
        steps = jnp.exp(jax.random.uniform(jax.random.fold_in(own, position), (shards_of,), jnp.float32, low / len(shards), largest / len(shards)))
        loudness = loudness * jnp.repeat(steps, dims[position] // shards_of).reshape([-1 if axis == position else 1 for axis in range(len(dims))])
    return loudness


def gaussian(rng, extent, width, reach, pieces=(), held_as=jnp.bfloat16):
    values = width * jax.random.normal(rng, extent, jnp.float32)
    if pieces:
        values = values * levels(rng, extent, pieces, -0.22, 0.18)
    return jnp.clip(values, -reach, reach).astype(held_as)


def setup_inputs(seed: int = 0) -> dict:
    seeds = jax.random.split(jax.random.key(seed), 7)
    return {
        "weight": gaussian(seeds[0], (D, FF), 1.0, 6.0, ((0, 16), (1, 32))),
        "gradient": gaussian(seeds[1], (D, FF), 1.0, 6.0, ((0, 16), (1, 32))),
        "old_basis": gaussian(seeds[2], (D, RANK), D ** -0.5, 0.0625, ((0, 16),)),
        "new_basis": gaussian(seeds[3], (D, RANK), D ** -0.5, 0.0625, ((0, 16),)),
        "first_moment": gaussian(seeds[4], (RANK, FF), 1.0, 6.0, ((1, 512),), jnp.float32),
        "second_moment": jnp.clip(jnp.exp(math.log(2.0) - 3.6888794 * jax.random.uniform(seeds[5], (RANK, FF), jnp.float32) ** levels(seeds[5], (RANK, FF), ((1, 512),), -0.2, 0.2)), 0.05, 2.0),
    }


beta_first = 0.9
beta_second = 0.95
epsilon = 1e-08
step_rate = 0.0025

def reference(weight, gradient, old_basis, new_basis, first_moment, second_moment):
    transition = jnp.dot(new_basis.T, old_basis, preferred_element_type=jnp.float32)
    projected = jnp.dot(new_basis.T, gradient, preferred_element_type=jnp.float32)
    moved_first = jnp.dot(transition, first_moment, precision=lax.Precision.HIGHEST)
    moved_second = jnp.dot(transition * transition, second_moment, precision=lax.Precision.HIGHEST)
    first_new = beta_first * moved_first + (1.0 - beta_first) * projected
    second_new = beta_second * moved_second + (1.0 - beta_second) * projected * projected
    direction = (first_new / (jnp.sqrt(second_new) + epsilon)).astype(jnp.bfloat16)
    back = jnp.dot(new_basis, direction, preferred_element_type=jnp.float32)
    new_weight = (weight.astype(jnp.float32) - step_rate * back).astype(jnp.bfloat16)
    return (new_weight, back.astype(jnp.bfloat16), first_new, second_new)
```

```python
import jax
import jax.numpy as jnp
from jax import lax
from jax.sharding import Mesh, PartitionSpec as P

beta_first = 0.9
beta_second = 0.95
epsilon = 1e-08
step_rate = 0.0025

names = ("yh", "x", "c", "z", "yl")
chips = ("yh", "x")
f32 = jnp.float32
bf16 = jnp.bfloat16


def swapped(value, axis):
    return lax.ppermute(value, axis, [(i, i ^ 1) for i in range(lax.axis_size(axis))])


def in_order(own, other, bit, dim):
    return jnp.where(
        bit == 0, jnp.concatenate([own, other], dim), jnp.concatenate([other, own], dim)
    )


def exchanged(value):
    return lax.all_to_all(value, chips, 0, 0, tiled=True)


def shards(weight, gradient, old_basis, new_basis, first_moment, second_moment):
    ranks = new_basis.shape[1]
    n_chips = lax.axis_size("yh") * lax.axis_size("x")
    per_chip = ranks // n_chips
    columns = gradient.shape[1]
    own_columns = first_moment.shape[1]
    half = columns // 2
    core = lax.axis_index("c")
    z_bit = lax.axis_index("z") & 1
    y_bit = lax.axis_index("yl")
    quarter = ranks // 4
    eighth = ranks // 8

    old_part = lax.dynamic_slice_in_dim(old_basis, (z_bit * 2 + y_bit) * quarter, quarter, 1)
    grad_t = jnp.einsum("dn,dr->nr", gradient, new_basis, preferred_element_type=f32)
    trans_t = jnp.einsum("dk,dr->kr", old_part, new_basis, preferred_element_type=f32)
    grad_t = grad_t.reshape(n_chips, 2, own_columns, n_chips, per_chip)
    trans_t = trans_t.reshape(2, eighth, n_chips, per_chip)

    def for_core(which):
        g = lax.dynamic_index_in_dim(grad_t, which, 1, keepdims=False)
        t = lax.dynamic_index_in_dim(trans_t, which, 0, keepdims=False)
        g = g.transpose(2, 0, 1, 3).reshape(n_chips, half, per_chip)
        return jnp.concatenate([g, t.transpose(1, 0, 2)], 1)

    theirs = swapped(for_core(1 - core).astype(bf16), "c")
    pair = (for_core(core) + theirs.astype(f32)).astype(bf16)
    pieces = exchanged(pair)
    both = jnp.concatenate([first_moment.T, second_moment.T], 0).astype(bf16)
    both, pieces = lax.optimization_barrier((both, pieces))
    moments = exchanged(jnp.broadcast_to(both[None], (n_chips, *both.shape)))
    total = pieces.astype(f32).sum(0)
    projected = total[:half]
    trans = total[half:]
    trans = in_order(trans, swapped(trans, "c"), core, 0)
    trans = in_order(trans, swapped(trans, "yl"), y_bit, 0)
    trans = in_order(trans, swapped(trans, "z"), z_bit, 0)
    first_t = moments[:, :own_columns].reshape(half, ranks)
    second_t = moments[:, own_columns:].reshape(half, ranks)

    def product(left, right):
        return jnp.dot(left, right, preferred_element_type=f32)

    high = lax.reduce_precision(trans, 8, 7)
    moved_first = product(first_t, high.astype(bf16)) + product(first_t, (trans - high).astype(bf16))
    moved_second = product(second_t, (trans * trans).astype(bf16))
    first_new = beta_first * moved_first + (1.0 - beta_first) * projected
    second_new = beta_second * moved_second + (1.0 - beta_second) * projected * projected
    direction = (first_new / (jnp.sqrt(second_new) + epsilon)).astype(bf16)
    out = jnp.concatenate(
        [
            jnp.broadcast_to(direction[None], (n_chips, half, per_chip)),
            first_new.astype(bf16).reshape(n_chips, own_columns, per_chip),
            second_new.astype(bf16).reshape(n_chips, own_columns, per_chip),
        ],
        1,
    )
    arrived = exchanged(out)
    own = arrived[:, :half]
    other = swapped(own, "c")
    dirs = in_order(
        own.reshape(n_chips, n_chips, 1, own_columns, per_chip),
        other.reshape(n_chips, n_chips, 1, own_columns, per_chip),
        core,
        2,
    )
    dirs = dirs.transpose(1, 2, 3, 0, 4).reshape(columns, ranks)
    back = jnp.einsum("dr,nr->dn", new_basis, dirs, preferred_element_type=f32)
    new_weight = (weight.astype(f32) - step_rate * back).astype(bf16)

    def whole(block):
        return block.transpose(1, 0, 2).reshape(own_columns, ranks).astype(f32).T

    return (
        new_weight,
        back.astype(bf16),
        whole(arrived[:, half : half + own_columns]),
        whole(arrived[:, half + own_columns :]),
    )


def solution(mesh):
    fine = Mesh(mesh.devices.reshape(2, 4, 2, mesh.shape["col"] // 2, 2), names)
    row, col = ("yh", "x", "c"), ("z", "yl")
    split = P(row, col)
    moments = P(None, col + row)
    return jax.shard_map(
        shards,
        mesh=fine,
        in_specs=(split, split, P(row, None), P(row, None), moments, moments),
        out_specs=(split, split, moments, moments),
        check_vma=False,
    )
```

```python
import jax
import jax.numpy as jnp
from jax import lax
from jax.experimental import pallas as pl
from jax.experimental.pallas import tpu as pltpu
from jax.sharding import Mesh, PartitionSpec as P

beta_first = 0.9
beta_second = 0.95
epsilon = 1e-08
step_rate = 0.0025

names = ("yh", "x", "c", "z", "yl")
chips = ("yh", "x")
row = ("yh", "x", "c")
col = ("z", "yl")
f32 = jnp.float32
bf16 = jnp.bfloat16


def swapped(value, axis):
    return lax.ppermute(value, axis, [(0, 1), (1, 0)])


def turned(value, axis, step):
    size = lax.axis_size(axis)

    def source(i):
        return i - i % 4 + (i + step) % 4

    return lax.ppermute(value, axis, [(source(i), i) for i in range(size)])


def chosen(values, which):
    out = values[0]
    for place in range(1, len(values)):
        out = jnp.where(which == place, values[place], out)
    return out


def exchanged(value):
    return lax.all_to_all(value, chips, 0, 0, tiled=True)


def transposed_product(left, right):
    return lax.dot_general(left, right, (((0,), (0,)), ((), ())), preferred_element_type=f32)


def products_kernel(
    place_ref, old_ref, grad_ref, new_ref, trans_ref, mine_ref, theirs_ref, total
):
    part = transposed_product(old_ref[...], new_ref[...])
    blocks, rows, per_chip = trans_ref.shape
    for block in range(blocks):
        chip, core = block // 2, block % 2
        piece = part[core * rows : (core + 1) * rows, chip * per_chip : (chip + 1) * per_chip]
        trans_ref[block] = piece.astype(trans_ref.dtype)
    total[...] = transposed_product(grad_ref[...], new_ref[...])
    n_chips, rows, _ = mine_ref.shape
    core = place_ref[1]
    for out_ref, which in ((theirs_ref, 1 - core), (mine_ref, core)):
        for block in range(n_chips):
            start = pl.multiple_of((2 * block + which) * rows, rows)
            part = total[pl.ds(start, rows), :]
            for chip in range(n_chips):
                out_ref[chip, :, block * per_chip : (block + 1) * per_chip] = part[
                    :, chip * per_chip : (chip + 1) * per_chip
                ].astype(out_ref.dtype)


def products(place, old_basis, gradient, new_basis, n_chips, own_columns):
    depth, ranks = new_basis.shape
    columns = gradient.shape[1]
    quarter = ranks // 4
    trans = jax.ShapeDtypeStruct((2 * n_chips, quarter // 2, ranks // n_chips), bf16)
    dims = (n_chips, own_columns, ranks)

    def whole(shape):
        return pl.BlockSpec(shape, lambda i, place: (0,) * len(shape))

    return pl.pallas_call(
        products_kernel,
        out_shape=(
            trans,
            jax.ShapeDtypeStruct(dims, f32),
            jax.ShapeDtypeStruct(dims, bf16),
        ),
        grid_spec=pltpu.PrefetchScalarGridSpec(
            num_scalar_prefetch=1,
            grid=(1,),
            in_specs=[
                pl.BlockSpec((depth, quarter), lambda i, place: (0, place[0])),
                whole((depth, columns)),
                whole((depth, ranks)),
            ],
            out_specs=(whole(trans.shape), whole(dims), whole(dims)),
            scratch_shapes=[pltpu.VMEM((columns, ranks), f32)],
        ),
        compiler_params=pltpu.CompilerParams(vmem_limit_bytes=24 * 2**20),
        cost_estimate=pl.CostEstimate(
            flops=2 * depth * (columns + quarter) * ranks,
            bytes_accessed=5 * 2**20,
            transcendentals=0,
        ),
    )(place, old_basis, gradient, new_basis)


def back_kernel(core_ref, own_ref, other_ref, new_ref, weight_ref, new_weight_ref, update_ref, dirs):
    @pl.when(pl.program_id(0) == 0)
    def _():
        n_chips, half, width = other_ref.shape
        rows = half // n_chips
        core = core_ref[0]
        for ref, which in ((own_ref, core), (other_ref, 1 - core)):
            for block in range(n_chips):
                start = pl.multiple_of((2 * block + which) * rows, rows)
                for chip in range(n_chips):
                    dirs[pl.ds(start, rows), chip * width : (chip + 1) * width] = ref[
                        chip, block * rows : (block + 1) * rows, :
                    ]

    back = lax.dot_general(
        new_ref[...], dirs[...], (((1,), (1,)), ((), ())), preferred_element_type=f32
    )
    update_ref[...] = back.astype(bf16)
    new_weight_ref[...] = (weight_ref[...].astype(f32) - step_rate * back).astype(bf16)


def stepped(core, arrived, other, new_basis, weight):
    depth, ranks = new_basis.shape
    columns = weight.shape[1]
    steps = 2
    rows = depth // steps
    out = jax.ShapeDtypeStruct(weight.shape, bf16)
    block = pl.BlockSpec((rows, columns), lambda i, core: (i, 0))
    return pl.pallas_call(
        back_kernel,
        out_shape=(out, out),
        grid_spec=pltpu.PrefetchScalarGridSpec(
            num_scalar_prefetch=1,
            grid=(steps,),
            in_specs=[
                pl.BlockSpec(arrived.shape, lambda i, core: (0, 0, 0)),
                pl.BlockSpec(other.shape, lambda i, core: (0, 0, 0)),
                pl.BlockSpec((rows, ranks), lambda i, core: (i, 0)),
                block,
            ],
            out_specs=(block, block),
            scratch_shapes=[pltpu.VMEM((columns, ranks), bf16)],
        ),
        compiler_params=pltpu.CompilerParams(vmem_limit_bytes=24 * 2**20),
        cost_estimate=pl.CostEstimate(
            flops=2 * depth * columns * ranks, bytes_accessed=5 * 2**20, transcendentals=0
        ),
    )(core, arrived, other, new_basis, weight)


def shards(weight, gradient, old_basis, new_basis, first_moment, second_moment):
    ranks = new_basis.shape[1]
    n_chips = lax.axis_size("yh") * lax.axis_size("x")
    per_chip = ranks // n_chips
    columns = gradient.shape[1]
    own_columns = first_moment.shape[1]
    half = columns // 2
    core = lax.axis_index("c")

    residue = lax.axis_index("z") % 4
    which = core.reshape(1)
    pieces, mine, theirs = products(
        jnp.stack([residue, core]), old_basis, gradient, new_basis, n_chips, own_columns
    )
    pieces = lax.all_to_all(pieces, row, 0, 0, tiled=True)
    pair = (mine + swapped(theirs, "c").astype(f32)).astype(bf16)
    both = jnp.concatenate([first_moment.T, second_moment.T], 0).astype(bf16)
    both = jnp.broadcast_to(both[None], (n_chips, *both.shape))
    packed = jnp.concatenate([pair, both], 1)
    packed, pieces = lax.optimization_barrier((packed, pieces))
    packed = exchanged(packed)

    trans = pieces.astype(f32).sum(0)
    quarters = [trans] + [turned(trans, "z", step) for step in (1, 2, 3)]
    trans = jnp.stack([chosen(quarters, (place - residue) % 4) for place in range(4)])
    other = swapped(trans, "c")
    trans = jnp.where(core == 0, jnp.stack([trans, other], 1), jnp.stack([other, trans], 1))
    trans = trans.reshape(ranks, per_chip)

    projected = packed[:, :own_columns].astype(f32).sum(0)
    projected = projected.reshape(own_columns, n_chips, per_chip).transpose(1, 0, 2)
    projected = projected.reshape(half, per_chip)
    first_t = packed[:, own_columns : 2 * own_columns].reshape(half, ranks)
    second_t = packed[:, 2 * own_columns :].reshape(half, ranks)

    def product(left, right):
        return jnp.dot(left, right, preferred_element_type=f32)

    high = lax.reduce_precision(trans, 8, 7)
    moved_first = product(first_t, high.astype(bf16)) + product(first_t, (trans - high).astype(bf16))
    moved_second = product(second_t, (trans * trans).astype(bf16))
    first_new = beta_first * moved_first + (1.0 - beta_first) * projected
    second_new = beta_second * moved_second + (1.0 - beta_second) * projected * projected
    direction = (first_new / (jnp.sqrt(second_new) + epsilon)).astype(bf16)
    out = jnp.concatenate(
        [
            jnp.broadcast_to(direction[None], (n_chips, half, per_chip)),
            first_new.astype(bf16).reshape(n_chips, own_columns, per_chip),
            second_new.astype(bf16).reshape(n_chips, own_columns, per_chip),
        ],
        1,
    )
    arrived = exchanged(out)
    other = swapped(arrived[:, :half], "c")
    new_weight, update = stepped(which, arrived, other, new_basis, weight)

    def whole(block):
        return block.transpose(1, 0, 2).reshape(own_columns, ranks).astype(f32).T

    return (
        new_weight,
        update,
        whole(arrived[:, half : half + own_columns]),
        whole(arrived[:, half + own_columns :]),
    )


def solution(mesh):
    fine = Mesh(mesh.devices.reshape(2, 4, 2, mesh.shape["col"] // 2, 2), names)
    split = P(row, col)
    moments = P(None, col + row)
    return jax.shard_map(
        shards,
        mesh=fine,
        in_specs=(split, split, P(row, None), P(row, None), moments, moments),
        out_specs=(split, split, moments, moments),
        check_vma=False,
    )
```

```python
import jax
import jax.numpy as jnp
from jax import lax
from jax.experimental import pallas as pl
from jax.experimental.pallas import tpu as pltpu
from jax.sharding import Mesh, PartitionSpec as P

beta_first = 0.9
beta_second = 0.95
epsilon = 1e-08
step_rate = 0.0025

names = ("yh", "x", "c", "z", "yl")
chips = ("yh", "x")
row = ("yh", "x", "c")
col = ("z", "yl")
f32 = jnp.float32
bf16 = jnp.bfloat16


def swapped(value, axis):
    return lax.ppermute(value, axis, [(0, 1), (1, 0)])


def turned(value, axis, step):
    size = lax.axis_size(axis)

    def source(i):
        return i - i % 4 + (i + step) % 4

    return lax.ppermute(value, axis, [(source(i), i) for i in range(size)])


def chosen(values, which):
    out = values[0]
    for place in range(1, len(values)):
        out = jnp.where(which == place, values[place], out)
    return out


def exchanged(value):
    return lax.all_to_all(value, chips, 0, 0, tiled=True)


def transposed_product(left, right):
    return lax.dot_general(left, right, (((0,), (0,)), ((), ())), preferred_element_type=f32)


def products_kernel(
    place_ref, old_ref, grad_ref, new_ref, trans_ref, mine_ref, theirs_ref, total
):
    part = transposed_product(old_ref[...], new_ref[...])
    blocks, rows, per_chip = trans_ref.shape
    for block in range(blocks):
        chip, core = block // 2, block % 2
        piece = part[core * rows : (core + 1) * rows, chip * per_chip : (chip + 1) * per_chip]
        trans_ref[block] = piece.astype(trans_ref.dtype)
    total[...] = transposed_product(grad_ref[...], new_ref[...])
    n_chips, rows, _ = mine_ref.shape
    core = place_ref[1]
    for out_ref, which in ((theirs_ref, 1 - core), (mine_ref, core)):
        for block in range(n_chips):
            start = pl.multiple_of((2 * block + which) * rows, rows)
            part = total[pl.ds(start, rows), :]
            for chip in range(n_chips):
                out_ref[chip, :, block * per_chip : (block + 1) * per_chip] = part[
                    :, chip * per_chip : (chip + 1) * per_chip
                ].astype(out_ref.dtype)


def products(place, old_basis, gradient, new_basis, n_chips, own_columns):
    depth, ranks = new_basis.shape
    columns = gradient.shape[1]
    quarter = ranks // 4
    trans = jax.ShapeDtypeStruct((2 * n_chips, quarter // 2, ranks // n_chips), bf16)
    dims = (n_chips, own_columns, ranks)

    def whole(shape):
        return pl.BlockSpec(shape, lambda i, place: (0,) * len(shape))

    return pl.pallas_call(
        products_kernel,
        out_shape=(
            trans,
            jax.ShapeDtypeStruct(dims, f32),
            jax.ShapeDtypeStruct(dims, bf16),
        ),
        grid_spec=pltpu.PrefetchScalarGridSpec(
            num_scalar_prefetch=1,
            grid=(1,),
            in_specs=[
                pl.BlockSpec((depth, quarter), lambda i, place: (0, place[0])),
                whole((depth, columns)),
                whole((depth, ranks)),
            ],
            out_specs=(whole(trans.shape), whole(dims), whole(dims)),
            scratch_shapes=[pltpu.VMEM((columns, ranks), f32)],
        ),
        compiler_params=pltpu.CompilerParams(vmem_limit_bytes=60 * 2**20),
        cost_estimate=pl.CostEstimate(
            flops=2 * depth * (columns + quarter) * ranks,
            bytes_accessed=5 * 2**20,
            transcendentals=0,
        ),
    )(place, old_basis, gradient, new_basis)


def back_kernel(core_ref, own_ref, other_ref, new_ref, weight_ref, new_weight_ref, update_ref, dirs):
    @pl.when(pl.program_id(0) == 0)
    def _():
        n_chips, half, width = other_ref.shape
        rows = half // n_chips
        core = core_ref[0]
        for ref, which in ((own_ref, core), (other_ref, 1 - core)):
            for block in range(n_chips):
                start = pl.multiple_of((2 * block + which) * rows, rows)
                for chip in range(n_chips):
                    dirs[pl.ds(start, rows), chip * width : (chip + 1) * width] = ref[
                        chip, block * rows : (block + 1) * rows, :
                    ]

    back = lax.dot_general(
        new_ref[...], dirs[...], (((1,), (1,)), ((), ())), preferred_element_type=f32
    )
    update_ref[...] = back.astype(bf16)
    new_weight_ref[...] = (weight_ref[...].astype(f32) - step_rate * back).astype(bf16)


def stepped(core, arrived, other, new_basis, weight):
    depth, ranks = new_basis.shape
    columns = weight.shape[1]
    steps = 2
    rows = depth // steps
    out = jax.ShapeDtypeStruct(weight.shape, bf16)
    block = pl.BlockSpec((rows, columns), lambda i, core: (i, 0))
    return pl.pallas_call(
        back_kernel,
        out_shape=(out, out),
        grid_spec=pltpu.PrefetchScalarGridSpec(
            num_scalar_prefetch=1,
            grid=(steps,),
            in_specs=[
                pl.BlockSpec(arrived.shape, lambda i, core: (0, 0, 0)),
                pl.BlockSpec(other.shape, lambda i, core: (0, 0, 0)),
                pl.BlockSpec((rows, ranks), lambda i, core: (i, 0)),
                block,
            ],
            out_specs=(block, block),
            scratch_shapes=[pltpu.VMEM((columns, ranks), bf16)],
        ),
        compiler_params=pltpu.CompilerParams(vmem_limit_bytes=24 * 2**20),
        cost_estimate=pl.CostEstimate(
            flops=2 * depth * columns * ranks, bytes_accessed=5 * 2**20, transcendentals=0
        ),
    )(core, arrived, other, new_basis, weight)


def shards(weight, gradient, old_basis, new_basis, first_moment, second_moment):
    ranks = new_basis.shape[1]
    n_chips = lax.axis_size("yh") * lax.axis_size("x")
    per_chip = ranks // n_chips
    columns = gradient.shape[1]
    own_columns = first_moment.shape[1]
    half = columns // 2
    core = lax.axis_index("c")

    residue = lax.axis_index("z") % 4
    which = core.reshape(1)
    pieces, mine, theirs = products(
        jnp.stack([residue, core]), old_basis, gradient, new_basis, n_chips, own_columns
    )
    pieces = lax.all_to_all(pieces, row, 0, 0, tiled=True)
    pair = (mine + swapped(theirs, "c").astype(f32)).astype(bf16)
    both = jnp.concatenate([first_moment.T, second_moment.T], 0).astype(bf16)
    both = jnp.broadcast_to(both[None], (n_chips, *both.shape))
    packed = jnp.concatenate([pair, both], 1)
    packed, pieces = lax.optimization_barrier((packed, pieces))
    packed = exchanged(packed)

    trans = pieces.astype(f32).sum(0)
    quarters = [trans] + [turned(trans, "z", step) for step in (1, 2, 3)]
    trans = jnp.stack([chosen(quarters, (place - residue) % 4) for place in range(4)])
    other = swapped(trans, "c")
    trans = jnp.where(core == 0, jnp.stack([trans, other], 1), jnp.stack([other, trans], 1))
    trans = trans.reshape(ranks, per_chip)

    projected = packed[:, :own_columns].astype(f32).sum(0)
    projected = projected.reshape(own_columns, n_chips, per_chip).transpose(1, 0, 2)
    projected = projected.reshape(half, per_chip)
    first_t = packed[:, own_columns : 2 * own_columns].reshape(half, ranks)
    second_t = packed[:, 2 * own_columns :].reshape(half, ranks)

    def product(left, right):
        return jnp.dot(left, right, preferred_element_type=f32)

    high = lax.reduce_precision(trans, 8, 7)
    moved_first = product(first_t, high.astype(bf16)) + product(first_t, (trans - high).astype(bf16))
    moved_second = product(second_t, (trans * trans).astype(bf16))
    first_new = beta_first * moved_first + (1.0 - beta_first) * projected
    second_new = beta_second * moved_second + (1.0 - beta_second) * projected * projected
    direction = (first_new / (jnp.sqrt(second_new) + epsilon)).astype(bf16)
    out = jnp.concatenate(
        [
            jnp.broadcast_to(direction[None], (n_chips, half, per_chip)),
            first_new.astype(bf16).reshape(n_chips, own_columns, per_chip),
            second_new.astype(bf16).reshape(n_chips, own_columns, per_chip),
        ],
        1,
    )
    arrived = exchanged(out)
    other = swapped(arrived[:, :half], "c")
    new_weight, update = stepped(which, arrived, other, new_basis, weight)

    def whole(block):
        return block.transpose(1, 0, 2).reshape(own_columns, ranks).astype(f32).T

    return (
        new_weight,
        update,
        whole(arrived[:, half : half + own_columns]),
        whole(arrived[:, half + own_columns :]),
    )


def solution(mesh):
    fine = Mesh(mesh.devices.reshape(2, 4, 2, mesh.shape["col"] // 2, 2), names)
    split = P(row, col)
    moments = P(None, col + row)
    return jax.shard_map(
        shards,
        mesh=fine,
        in_specs=(split, split, P(row, None), P(row, None), moments, moments),
        out_specs=(split, split, moments, moments),
        check_vma=False,
    )
```

```python
import jax
import jax.numpy as jnp
from jax import lax
from jax.experimental import pallas as pl
from jax.experimental.pallas import tpu as pltpu
from jax.sharding import Mesh, PartitionSpec as P

beta_first = 0.9
beta_second = 0.95
epsilon = 1e-08
step_rate = 0.0025

names = ("yh", "x", "c", "z", "yl")
chips = ("yh", "x")
row = ("yh", "x", "c")
col = ("z", "yl")
vmem = 24 * 2**20
f32 = jnp.float32
bf16 = jnp.bfloat16


def swapped(value, axis):
    return lax.ppermute(value, axis, [(0, 1), (1, 0)])


def turned(value, axis, step):
    size = lax.axis_size(axis)

    def source(i):
        return i - i % 4 + (i + step) % 4

    return lax.ppermute(value, axis, [(source(i), i) for i in range(size)])


def chosen(values, which):
    out = values[0]
    for place in range(1, len(values)):
        out = jnp.where(which == place, values[place], out)
    return out


def exchanged(value):
    return lax.all_to_all(value, chips, 0, 0, tiled=True)


def transposed_product(left, right):
    return lax.dot_general(left, right, (((0,), (0,)), ((), ())), preferred_element_type=f32)


def whole(shape):
    return pl.BlockSpec(shape, lambda i, place: (0,) * len(shape))


def trans_kernel(place_ref, old_ref, new_ref, trans_ref):
    part = transposed_product(old_ref[...], new_ref[...])
    blocks, rows, per_chip = trans_ref.shape
    for block in range(blocks):
        chip, core = block // 2, block % 2
        piece = part[core * rows : (core + 1) * rows, chip * per_chip : (chip + 1) * per_chip]
        trans_ref[block] = piece.astype(trans_ref.dtype)


def trans_pieces(place, old_basis, new_basis, n_chips):
    depth, ranks = new_basis.shape
    quarter = ranks // 4
    steps = 2
    dims = (2 * n_chips, quarter // 2, ranks // n_chips)
    return pl.pallas_call(
        trans_kernel,
        out_shape=jax.ShapeDtypeStruct(dims, bf16),
        grid_spec=pltpu.PrefetchScalarGridSpec(
            num_scalar_prefetch=1,
            grid=(steps,),
            in_specs=[
                pl.BlockSpec((depth, quarter), lambda i, place: (0, place[0])),
                pl.BlockSpec((depth, ranks // steps), lambda i, place: (0, i)),
            ],
            out_specs=pl.BlockSpec((dims[0] // steps, *dims[1:]), lambda i, place: (i, 0, 0)),
        ),
        compiler_params=pltpu.CompilerParams(vmem_limit_bytes=60 * 2**20),
        cost_estimate=pl.CostEstimate(
            flops=2 * depth * quarter * ranks, bytes_accessed=2 * 2**20, transcendentals=0
        ),
    )(place, old_basis, new_basis)


def grad_kernel(core_ref, grad_ref, new_ref, mine_ref, low_ref, high_ref, total):
    total[...] = transposed_product(grad_ref[...], new_ref[...])
    n_chips, rows, ranks = mine_ref.shape
    per_chip = ranks // n_chips
    half = n_chips // 2
    core = core_ref[0]
    for block in range(n_chips):
        lanes = slice(block * per_chip, (block + 1) * per_chip)
        for own in (False, True):
            which = core if own else 1 - core
            start = pl.multiple_of((2 * block + which) * rows, rows)
            part = total[pl.ds(start, rows), :]
            for chip in range(n_chips):
                piece = part[:, chip * per_chip : (chip + 1) * per_chip]
                if own:
                    mine_ref[chip, :, lanes] = piece
                elif chip < half:
                    low_ref[chip, :, lanes] = piece.astype(bf16)
                else:
                    high_ref[chip - half, :, lanes] = piece.astype(bf16)


def grad_pieces(core, gradient, new_basis, n_chips, own_columns):
    depth, ranks = new_basis.shape
    columns = gradient.shape[1]
    dims = (n_chips, own_columns, ranks)
    part = (n_chips // 2, own_columns, ranks)
    return pl.pallas_call(
        grad_kernel,
        out_shape=(
            jax.ShapeDtypeStruct(dims, f32),
            jax.ShapeDtypeStruct(part, bf16),
            jax.ShapeDtypeStruct(part, bf16),
        ),
        grid_spec=pltpu.PrefetchScalarGridSpec(
            num_scalar_prefetch=1,
            grid=(1,),
            in_specs=[whole((depth, columns)), whole((depth, ranks))],
            out_specs=(whole(dims), whole(part), whole(part)),
            scratch_shapes=[pltpu.VMEM((columns, ranks), f32)],
        ),
        compiler_params=pltpu.CompilerParams(vmem_limit_bytes=vmem),
        cost_estimate=pl.CostEstimate(
            flops=2 * depth * columns * ranks, bytes_accessed=4 * 2**20, transcendentals=0
        ),
    )(core, gradient, new_basis)


def pack_kernel(mine_ref, low_ref, high_ref, first_ref, second_ref, out_ref):
    rows = first_ref.shape[0]
    n_chips = out_ref.shape[0]
    half = n_chips // 2
    both = jnp.concatenate([first_ref[...], second_ref[...]], 0).astype(bf16)
    for chip in range(n_chips):
        theirs = low_ref[chip] if chip < half else high_ref[chip - half]
        out_ref[chip, :rows] = (mine_ref[chip] + theirs.astype(f32)).astype(bf16)
        out_ref[chip, rows:] = both


def packed_for(mine, low, high, first_t, second_t):
    n_chips, rows, ranks = mine.shape
    return pl.pallas_call(
        pack_kernel,
        out_shape=jax.ShapeDtypeStruct((n_chips, 3 * rows, ranks), bf16),
        compiler_params=pltpu.CompilerParams(vmem_limit_bytes=vmem),
        cost_estimate=pl.CostEstimate(flops=1, bytes_accessed=1, transcendentals=0),
    )(mine, low, high, first_t, second_t)


def back_kernel(core_ref, own_ref, other_ref, new_ref, weight_ref, new_weight_ref, update_ref, dirs):
    @pl.when(pl.program_id(0) == 0)
    def _():
        n_chips, half, width = other_ref.shape
        rows = half // n_chips
        core = core_ref[0]
        for ref, which in ((own_ref, core), (other_ref, 1 - core)):
            for block in range(n_chips):
                start = pl.multiple_of((2 * block + which) * rows, rows)
                for chip in range(n_chips):
                    dirs[pl.ds(start, rows), chip * width : (chip + 1) * width] = ref[
                        chip, block * rows : (block + 1) * rows, :
                    ]

    back = lax.dot_general(
        new_ref[...], dirs[...], (((1,), (1,)), ((), ())), preferred_element_type=f32
    )
    update_ref[...] = back.astype(bf16)
    new_weight_ref[...] = (weight_ref[...].astype(f32) - step_rate * back).astype(bf16)


def stepped(core, arrived, other, new_basis, weight):
    depth, ranks = new_basis.shape
    columns = weight.shape[1]
    steps = 2
    rows = depth // steps
    out = jax.ShapeDtypeStruct(weight.shape, bf16)
    block = pl.BlockSpec((rows, columns), lambda i, core: (i, 0))
    return pl.pallas_call(
        back_kernel,
        out_shape=(out, out),
        grid_spec=pltpu.PrefetchScalarGridSpec(
            num_scalar_prefetch=1,
            grid=(steps,),
            in_specs=[
                pl.BlockSpec(arrived.shape, lambda i, core: (0, 0, 0)),
                pl.BlockSpec(other.shape, lambda i, core: (0, 0, 0)),
                pl.BlockSpec((rows, ranks), lambda i, core: (i, 0)),
                block,
            ],
            out_specs=(block, block),
            scratch_shapes=[pltpu.VMEM((columns, ranks), bf16)],
        ),
        compiler_params=pltpu.CompilerParams(vmem_limit_bytes=24 * 2**20),
        cost_estimate=pl.CostEstimate(
            flops=2 * depth * columns * ranks, bytes_accessed=5 * 2**20, transcendentals=0
        ),
    )(core, arrived, other, new_basis, weight)


def shards(weight, gradient, old_basis, new_basis, first_moment, second_moment):
    ranks = new_basis.shape[1]
    n_chips = lax.axis_size("yh") * lax.axis_size("x")
    per_chip = ranks // n_chips
    columns = gradient.shape[1]
    own_columns = first_moment.shape[1]
    half = columns // 2
    core = lax.axis_index("c")

    residue = lax.axis_index("z") % 4
    pieces = trans_pieces(residue.reshape(1), old_basis, new_basis, n_chips)
    pieces, gradient = lax.optimization_barrier((pieces, gradient))
    pieces = lax.all_to_all(pieces, row, 0, 0, tiled=True)
    which = core.reshape(1)
    mine, low, high = grad_pieces(which, gradient, new_basis, n_chips, own_columns)
    low, high = swapped(low, "c"), swapped(high, "c")
    packed = packed_for(mine, low, high, first_moment.T, second_moment.T)
    packed, pieces = lax.optimization_barrier((packed, pieces))
    packed = exchanged(packed)

    trans = pieces.astype(f32).sum(0)
    quarters = [trans] + [turned(trans, "z", step) for step in (1, 2, 3)]
    trans = jnp.stack([chosen(quarters, (place - residue) % 4) for place in range(4)])
    other = swapped(trans, "c")
    trans = jnp.where(core == 0, jnp.stack([trans, other], 1), jnp.stack([other, trans], 1))
    trans = trans.reshape(ranks, per_chip)

    projected = packed[:, :own_columns].astype(f32).sum(0)
    projected = projected.reshape(own_columns, n_chips, per_chip).transpose(1, 0, 2)
    projected = projected.reshape(half, per_chip)
    first_t = packed[:, own_columns : 2 * own_columns].reshape(half, ranks)
    second_t = packed[:, 2 * own_columns :].reshape(half, ranks)

    def product(left, right):
        return jnp.dot(left, right, preferred_element_type=f32)

    high = lax.reduce_precision(trans, 8, 7)
    moved_first = product(first_t, high.astype(bf16)) + product(first_t, (trans - high).astype(bf16))
    moved_second = product(second_t, (trans * trans).astype(bf16))
    first_new = beta_first * moved_first + (1.0 - beta_first) * projected
    second_new = beta_second * moved_second + (1.0 - beta_second) * projected * projected
    direction = (first_new / (jnp.sqrt(second_new) + epsilon)).astype(bf16)
    out = jnp.concatenate(
        [
            jnp.broadcast_to(direction[None], (n_chips, half, per_chip)),
            first_new.astype(bf16).reshape(n_chips, own_columns, per_chip),
            second_new.astype(bf16).reshape(n_chips, own_columns, per_chip),
        ],
        1,
    )
    arrived = exchanged(out)
    other = swapped(arrived[:, :half], "c")
    new_weight, update = stepped(which, arrived, other, new_basis, weight)

    def joined(block):
        return block.transpose(1, 0, 2).reshape(own_columns, ranks).astype(f32).T

    return (
        new_weight,
        update,
        joined(arrived[:, half : half + own_columns]),
        joined(arrived[:, half + own_columns :]),
    )


def solution(mesh):
    fine = Mesh(mesh.devices.reshape(2, 4, 2, mesh.shape["col"] // 2, 2), names)
    split = P(row, col)
    moments = P(None, col + row)
    return jax.shard_map(
        shards,
        mesh=fine,
        in_specs=(split, split, P(row, None), P(row, None), moments, moments),
        out_specs=(split, split, moments, moments),
        check_vma=False,
    )
```

```python
import jax
import jax.numpy as jnp
from jax import lax
from jax.experimental import pallas as pl
from jax.experimental.pallas import tpu as pltpu
from jax.sharding import Mesh, PartitionSpec as P

beta_first = 0.9
beta_second = 0.95
epsilon = 1e-08
step_rate = 0.0025

names = ("yh", "x", "c", "z", "yl")
chips = ("yh", "x")
row = ("yh", "x", "c")
col = ("z", "yl")
vmem = 24 * 2**20
f32 = jnp.float32
bf16 = jnp.bfloat16


def swapped(value, axis):
    return lax.ppermute(value, axis, [(0, 1), (1, 0)])


def turned(value, axis, step):
    size = lax.axis_size(axis)

    def source(i):
        return i - i % 4 + (i + step) % 4

    return lax.ppermute(value, axis, [(source(i), i) for i in range(size)])


def chosen(values, which):
    out = values[0]
    for place in range(1, len(values)):
        out = jnp.where(which == place, values[place], out)
    return out


def exchanged(value):
    return lax.all_to_all(value, chips, 0, 0, tiled=True)


def transposed_product(left, right):
    return lax.dot_general(left, right, (((0,), (0,)), ((), ())), preferred_element_type=f32)


def whole(shape):
    return pl.BlockSpec(shape, lambda i, place: (0,) * len(shape))


def trans_kernel(place_ref, old_ref, new_ref, trans_ref):
    part = transposed_product(old_ref[...], new_ref[...])
    blocks, rows, per_chip = trans_ref.shape
    for block in range(blocks):
        chip, core = block // 2, block % 2
        piece = part[core * rows : (core + 1) * rows, chip * per_chip : (chip + 1) * per_chip]
        trans_ref[block] = piece.astype(trans_ref.dtype)


def trans_pieces(place, old_basis, new_basis, n_chips):
    depth, ranks = new_basis.shape
    quarter = ranks // 4
    steps = 2
    dims = (2 * n_chips, quarter // 2, ranks // n_chips)
    return pl.pallas_call(
        trans_kernel,
        out_shape=jax.ShapeDtypeStruct(dims, bf16),
        grid_spec=pltpu.PrefetchScalarGridSpec(
            num_scalar_prefetch=1,
            grid=(steps,),
            in_specs=[
                pl.BlockSpec((depth, quarter), lambda i, place: (0, place[0])),
                pl.BlockSpec((depth, ranks // steps), lambda i, place: (0, i)),
            ],
            out_specs=pl.BlockSpec((dims[0] // steps, *dims[1:]), lambda i, place: (i, 0, 0)),
        ),
        compiler_params=pltpu.CompilerParams(vmem_limit_bytes=60 * 2**20),
        cost_estimate=pl.CostEstimate(
            flops=2 * depth * quarter * ranks, bytes_accessed=2 * 2**20, transcendentals=0
        ),
    )(place, old_basis, new_basis)


def grad_kernel(core_ref, grad_ref, new_ref, mine_ref, low_ref, high_ref, total):
    total[...] = transposed_product(grad_ref[...], new_ref[...])
    n_chips, rows, ranks = mine_ref.shape
    per_chip = ranks // n_chips
    half = n_chips // 2
    core = core_ref[0]
    for block in range(n_chips):
        lanes = slice(block * per_chip, (block + 1) * per_chip)
        for own in (False, True):
            which = core if own else 1 - core
            start = pl.multiple_of((2 * block + which) * rows, rows)
            part = total[pl.ds(start, rows), :]
            for chip in range(n_chips):
                piece = part[:, chip * per_chip : (chip + 1) * per_chip]
                if own:
                    mine_ref[chip, :, lanes] = piece
                elif chip < half:
                    low_ref[chip, :, lanes] = piece.astype(bf16)
                else:
                    high_ref[chip - half, :, lanes] = piece.astype(bf16)


def grad_pieces(core, gradient, new_basis, n_chips, own_columns):
    depth, ranks = new_basis.shape
    columns = gradient.shape[1]
    dims = (n_chips, own_columns, ranks)
    part = (n_chips // 2, own_columns, ranks)
    return pl.pallas_call(
        grad_kernel,
        out_shape=(
            jax.ShapeDtypeStruct(dims, f32),
            jax.ShapeDtypeStruct(part, bf16),
            jax.ShapeDtypeStruct(part, bf16),
        ),
        grid_spec=pltpu.PrefetchScalarGridSpec(
            num_scalar_prefetch=1,
            grid=(1,),
            in_specs=[whole((depth, columns)), whole((depth, ranks))],
            out_specs=(whole(dims), whole(part), whole(part)),
            scratch_shapes=[pltpu.VMEM((columns, ranks), f32)],
        ),
        compiler_params=pltpu.CompilerParams(vmem_limit_bytes=vmem),
        cost_estimate=pl.CostEstimate(
            flops=2 * depth * columns * ranks, bytes_accessed=4 * 2**20, transcendentals=0
        ),
    )(core, gradient, new_basis)


def pack_kernel(mine_ref, low_ref, high_ref, first_ref, second_ref, out_ref):
    rows = first_ref.shape[0]
    n_chips = out_ref.shape[0]
    half = n_chips // 2
    both = jnp.concatenate([first_ref[...], second_ref[...]], 0).astype(bf16)
    for chip in range(n_chips):
        theirs = low_ref[chip] if chip < half else high_ref[chip - half]
        out_ref[chip, :rows] = (mine_ref[chip] + theirs.astype(f32)).astype(bf16)
        out_ref[chip, rows:] = both


def packed_for(mine, low, high, first_t, second_t):
    n_chips, rows, ranks = mine.shape
    return pl.pallas_call(
        pack_kernel,
        out_shape=jax.ShapeDtypeStruct((n_chips, 3 * rows, ranks), bf16),
        compiler_params=pltpu.CompilerParams(vmem_limit_bytes=vmem),
        cost_estimate=pl.CostEstimate(flops=1, bytes_accessed=1, transcendentals=0),
    )(mine, low, high, first_t, second_t)


def step_kernel(core_ref, own_ref, other_ref, packed_ref, out_ref, terms, squares):
    places, rows, per_chip = own_ref.shape
    core = core_ref[0]
    for ref, which in ((own_ref, core), (other_ref, 1 - core)):
        for place in range(places):
            start = pl.multiple_of((2 * place + which) * rows, rows)
            part = ref[place]
            high = part.astype(bf16)
            terms[pl.ds(start, rows), :per_chip] = high
            terms[pl.ds(start, rows), per_chip:] = (part - high.astype(f32)).astype(bf16)
            squares[pl.ds(start, rows), :] = (part * part).astype(bf16)
    n_chips, rows, ranks = packed_ref.shape
    rows = rows // 3
    half = n_chips * rows
    first_t = packed_ref[:, rows : 2 * rows, :].reshape(half, ranks)
    second_t = packed_ref[:, 2 * rows :, :].reshape(half, ranks)
    moved_first = jnp.dot(first_t, terms[...], preferred_element_type=f32)
    moved_first = moved_first[:, :per_chip] + moved_first[:, per_chip:]
    moved_second = jnp.dot(second_t, squares[...], preferred_element_type=f32)
    total = packed_ref[0, :rows, :].astype(f32)
    for chip in range(1, n_chips):
        total = total + packed_ref[chip, :rows, :].astype(f32)
    for block in range(n_chips):
        lines = slice(block * rows, (block + 1) * rows)
        projected = total[:, block * per_chip : (block + 1) * per_chip]
        first_new = beta_first * moved_first[lines] + (1.0 - beta_first) * projected
        second_new = beta_second * moved_second[lines] + (1.0 - beta_second) * projected * projected
        direction = (first_new / (jnp.sqrt(second_new) + epsilon)).astype(bf16)
        for chip in range(n_chips):
            out_ref[chip, lines, :] = direction
        out_ref[block, half : half + rows, :] = first_new.astype(bf16)
        out_ref[block, half + rows :, :] = second_new.astype(bf16)


def directions(core, own, other, packed):
    n_chips, rows, ranks = packed.shape
    rows = rows // 3
    per_chip = own.shape[2]
    dims = (n_chips, (n_chips + 2) * rows, per_chip)
    return pl.pallas_call(
        step_kernel,
        out_shape=jax.ShapeDtypeStruct(dims, bf16),
        grid_spec=pltpu.PrefetchScalarGridSpec(
            num_scalar_prefetch=1,
            grid=(1,),
            in_specs=[whole(own.shape), whole(other.shape), whole(packed.shape)],
            out_specs=whole(dims),
            scratch_shapes=[
                pltpu.VMEM((ranks, 2 * per_chip), bf16),
                pltpu.VMEM((ranks, per_chip), bf16),
            ],
        ),
        compiler_params=pltpu.CompilerParams(vmem_limit_bytes=vmem),
        cost_estimate=pl.CostEstimate(
            flops=6 * n_chips * rows * ranks * per_chip,
            bytes_accessed=3 * 2**20,
            transcendentals=2 * n_chips * rows * per_chip,
        ),
    )(core, own, other, packed)


def back_kernel(core_ref, own_ref, other_ref, new_ref, weight_ref, new_weight_ref, update_ref, dirs):
    @pl.when(pl.program_id(0) == 0)
    def _():
        n_chips, half, width = other_ref.shape
        rows = half // n_chips
        core = core_ref[0]
        for ref, which in ((own_ref, core), (other_ref, 1 - core)):
            for block in range(n_chips):
                start = pl.multiple_of((2 * block + which) * rows, rows)
                for chip in range(n_chips):
                    dirs[pl.ds(start, rows), chip * width : (chip + 1) * width] = ref[
                        chip, block * rows : (block + 1) * rows, :
                    ]

    back = lax.dot_general(
        new_ref[...], dirs[...], (((1,), (1,)), ((), ())), preferred_element_type=f32
    )
    update_ref[...] = back.astype(bf16)
    new_weight_ref[...] = (weight_ref[...].astype(f32) - step_rate * back).astype(bf16)


def stepped(core, arrived, other, new_basis, weight):
    depth, ranks = new_basis.shape
    columns = weight.shape[1]
    steps = 2
    rows = depth // steps
    out = jax.ShapeDtypeStruct(weight.shape, bf16)
    block = pl.BlockSpec((rows, columns), lambda i, core: (i, 0))
    return pl.pallas_call(
        back_kernel,
        out_shape=(out, out),
        grid_spec=pltpu.PrefetchScalarGridSpec(
            num_scalar_prefetch=1,
            grid=(steps,),
            in_specs=[
                pl.BlockSpec(arrived.shape, lambda i, core: (0, 0, 0)),
                pl.BlockSpec(other.shape, lambda i, core: (0, 0, 0)),
                pl.BlockSpec((rows, ranks), lambda i, core: (i, 0)),
                block,
            ],
            out_specs=(block, block),
            scratch_shapes=[pltpu.VMEM((columns, ranks), bf16)],
        ),
        compiler_params=pltpu.CompilerParams(vmem_limit_bytes=24 * 2**20),
        cost_estimate=pl.CostEstimate(
            flops=2 * depth * columns * ranks, bytes_accessed=5 * 2**20, transcendentals=0
        ),
    )(core, arrived, other, new_basis, weight)


def shards(weight, gradient, old_basis, new_basis, first_moment, second_moment):
    ranks = new_basis.shape[1]
    n_chips = lax.axis_size("yh") * lax.axis_size("x")
    per_chip = ranks // n_chips
    columns = gradient.shape[1]
    own_columns = first_moment.shape[1]
    half = columns // 2
    core = lax.axis_index("c")

    residue = lax.axis_index("z") % 4
    pieces = trans_pieces(residue.reshape(1), old_basis, new_basis, n_chips)
    pieces, gradient = lax.optimization_barrier((pieces, gradient))
    pieces = lax.all_to_all(pieces, row, 0, 0, tiled=True)
    which = core.reshape(1)
    mine, low, high = grad_pieces(which, gradient, new_basis, n_chips, own_columns)
    low, high = swapped(low, "c"), swapped(high, "c")
    packed = packed_for(mine, low, high, first_moment.T, second_moment.T)
    packed, pieces = lax.optimization_barrier((packed, pieces))
    packed = exchanged(packed)

    trans = pieces.astype(f32).sum(0)
    quarters = [trans] + [turned(trans, "z", step) for step in (1, 2, 3)]
    trans = jnp.stack([chosen(quarters, (place - residue) % 4) for place in range(4)])
    other = swapped(trans, "c")
    arrived = exchanged(directions(which, trans, other, packed))
    other = swapped(arrived[:, :half], "c")
    new_weight, update = stepped(which, arrived, other, new_basis, weight)

    def joined(block):
        return block.transpose(1, 0, 2).reshape(own_columns, ranks).astype(f32).T

    return (
        new_weight,
        update,
        joined(arrived[:, half : half + own_columns]),
        joined(arrived[:, half + own_columns :]),
    )


def solution(mesh):
    fine = Mesh(mesh.devices.reshape(2, 4, 2, mesh.shape["col"] // 2, 2), names)
    split = P(row, col)
    moments = P(None, col + row)
    return jax.shard_map(
        shards,
        mesh=fine,
        in_specs=(split, split, P(row, None), P(row, None), moments, moments),
        out_specs=(split, split, moments, moments),
        check_vma=False,
    )
```

```python
import jax
import jax.numpy as jnp
from jax import lax
from jax.experimental import pallas as pl
from jax.experimental.pallas import tpu as pltpu
from jax.sharding import Mesh, PartitionSpec as P

beta_first = 0.9
beta_second = 0.95
epsilon = 1e-08
step_rate = 0.0025

names = ("yh", "x", "c", "z", "yl")
chips = ("yh", "x")
row = ("yh", "x", "c")
col = ("z", "yl")
vmem = 24 * 2**20
f32 = jnp.float32
bf16 = jnp.bfloat16


def swapped(value, axis):
    return lax.ppermute(value, axis, [(0, 1), (1, 0)])


def turned(value, axis, step):
    size = lax.axis_size(axis)

    def source(i):
        return i - i % 4 + (i + step) % 4

    return lax.ppermute(value, axis, [(source(i), i) for i in range(size)])


def chosen(values, which):
    out = values[0]
    for place in range(1, len(values)):
        out = jnp.where(which == place, values[place], out)
    return out


def exchanged(value):
    return lax.all_to_all(value, chips, 0, 0, tiled=True)


def transposed_product(left, right):
    return lax.dot_general(left, right, (((0,), (0,)), ((), ())), preferred_element_type=f32)


def whole(shape):
    return pl.BlockSpec(shape, lambda i, place: (0,) * len(shape))


def trans_kernel(place_ref, old_ref, new_ref, trans_ref):
    part = transposed_product(old_ref[...], new_ref[...])
    blocks, rows, per_chip = trans_ref.shape
    for block in range(blocks):
        chip, core = block // 2, block % 2
        piece = part[core * rows : (core + 1) * rows, chip * per_chip : (chip + 1) * per_chip]
        trans_ref[block] = piece.astype(trans_ref.dtype)


def trans_pieces(place, old_basis, new_basis, n_chips):
    depth, ranks = new_basis.shape
    quarter = ranks // 4
    steps = 2
    dims = (2 * n_chips, quarter // 2, ranks // n_chips)
    return pl.pallas_call(
        trans_kernel,
        out_shape=jax.ShapeDtypeStruct(dims, bf16),
        grid_spec=pltpu.PrefetchScalarGridSpec(
            num_scalar_prefetch=1,
            grid=(steps,),
            in_specs=[
                pl.BlockSpec((depth, quarter), lambda i, place: (0, place[0])),
                pl.BlockSpec((depth, ranks // steps), lambda i, place: (0, i)),
            ],
            out_specs=pl.BlockSpec((dims[0] // steps, *dims[1:]), lambda i, place: (i, 0, 0)),
        ),
        compiler_params=pltpu.CompilerParams(vmem_limit_bytes=60 * 2**20),
        cost_estimate=pl.CostEstimate(
            flops=2 * depth * quarter * ranks, bytes_accessed=2 * 2**20, transcendentals=0
        ),
    )(place, old_basis, new_basis)


def grad_kernel(core_ref, grad_ref, new_ref, mine_ref, low_ref, high_ref, total):
    total[...] = transposed_product(grad_ref[...], new_ref[...])
    n_chips, rows, ranks = mine_ref.shape
    per_chip = ranks // n_chips
    half = n_chips // 2
    core = core_ref[0]
    for block in range(n_chips):
        lanes = slice(block * per_chip, (block + 1) * per_chip)
        for own in (False, True):
            which = core if own else 1 - core
            start = pl.multiple_of((2 * block + which) * rows, rows)
            part = total[pl.ds(start, rows), :]
            for chip in range(n_chips):
                piece = part[:, chip * per_chip : (chip + 1) * per_chip]
                if own:
                    mine_ref[chip, :, lanes] = piece
                elif chip < half:
                    low_ref[chip, :, lanes] = piece.astype(bf16)
                else:
                    high_ref[chip - half, :, lanes] = piece.astype(bf16)


def grad_pieces(core, gradient, new_basis, n_chips, own_columns):
    depth, ranks = new_basis.shape
    columns = gradient.shape[1]
    dims = (n_chips, own_columns, ranks)
    part = (n_chips // 2, own_columns, ranks)
    return pl.pallas_call(
        grad_kernel,
        out_shape=(
            jax.ShapeDtypeStruct(dims, f32),
            jax.ShapeDtypeStruct(part, bf16),
            jax.ShapeDtypeStruct(part, bf16),
        ),
        grid_spec=pltpu.PrefetchScalarGridSpec(
            num_scalar_prefetch=1,
            grid=(1,),
            in_specs=[whole((depth, columns)), whole((depth, ranks))],
            out_specs=(whole(dims), whole(part), whole(part)),
            scratch_shapes=[pltpu.VMEM((columns, ranks), f32)],
        ),
        compiler_params=pltpu.CompilerParams(vmem_limit_bytes=vmem),
        cost_estimate=pl.CostEstimate(
            flops=2 * depth * columns * ranks, bytes_accessed=4 * 2**20, transcendentals=0
        ),
    )(core, gradient, new_basis)


def pack_kernel(mine_ref, low_ref, high_ref, first_ref, second_ref, out_ref):
    rows = first_ref.shape[0]
    n_chips = out_ref.shape[0]
    half = n_chips // 2
    both = jnp.concatenate([first_ref[...], second_ref[...]], 0).astype(bf16)
    for chip in range(n_chips):
        theirs = low_ref[chip] if chip < half else high_ref[chip - half]
        out_ref[chip, :rows] = (mine_ref[chip] + theirs.astype(f32)).astype(bf16)
        out_ref[chip, rows:] = both


def packed_for(mine, low, high, first_t, second_t):
    n_chips, rows, ranks = mine.shape
    return pl.pallas_call(
        pack_kernel,
        out_shape=jax.ShapeDtypeStruct((n_chips, 3 * rows, ranks), bf16),
        compiler_params=pltpu.CompilerParams(vmem_limit_bytes=vmem),
        cost_estimate=pl.CostEstimate(flops=1, bytes_accessed=1, transcendentals=0),
    )(mine, low, high, first_t, second_t)


def step_kernel(core_ref, own_ref, other_ref, packed_ref, out_ref, terms, squares):
    places, rows, per_chip = own_ref.shape
    core = core_ref[0]
    for ref, which in ((own_ref, core), (other_ref, 1 - core)):
        for place in range(places):
            start = pl.multiple_of((2 * place + which) * rows, rows)
            part = ref[place]
            high = part.astype(bf16)
            terms[pl.ds(start, rows), :per_chip] = high
            terms[pl.ds(start, rows), per_chip:] = (part - high.astype(f32)).astype(bf16)
            squares[pl.ds(start, rows), :] = (part * part).astype(bf16)
    n_chips, rows, ranks = packed_ref.shape
    rows = rows // 3
    half = n_chips * rows
    first_t = packed_ref[:, rows : 2 * rows, :].reshape(half, ranks)
    second_t = packed_ref[:, 2 * rows :, :].reshape(half, ranks)
    moved_first = jnp.dot(first_t, terms[...], preferred_element_type=f32)
    moved_first = moved_first[:, :per_chip] + moved_first[:, per_chip:]
    moved_second = jnp.dot(second_t, squares[...], preferred_element_type=f32)
    total = packed_ref[0, :rows, :].astype(f32)
    for chip in range(1, n_chips):
        total = total + packed_ref[chip, :rows, :].astype(f32)
    for block in range(n_chips):
        lines = slice(block * rows, (block + 1) * rows)
        projected = total[:, block * per_chip : (block + 1) * per_chip]
        first_new = beta_first * moved_first[lines] + (1.0 - beta_first) * projected
        second_new = beta_second * moved_second[lines] + (1.0 - beta_second) * projected * projected
        direction = (first_new / (jnp.sqrt(second_new) + epsilon)).astype(bf16)
        for chip in range(n_chips):
            out_ref[chip, lines, :] = direction
        out_ref[block, half:, :] = second_new.astype(bf16)


def directions(core, own, other, packed):
    n_chips, rows, ranks = packed.shape
    rows = rows // 3
    per_chip = own.shape[2]
    dims = (n_chips, (n_chips + 1) * rows, per_chip)
    return pl.pallas_call(
        step_kernel,
        out_shape=jax.ShapeDtypeStruct(dims, bf16),
        grid_spec=pltpu.PrefetchScalarGridSpec(
            num_scalar_prefetch=1,
            grid=(1,),
            in_specs=[whole(own.shape), whole(other.shape), whole(packed.shape)],
            out_specs=whole(dims),
            scratch_shapes=[
                pltpu.VMEM((ranks, 2 * per_chip), bf16),
                pltpu.VMEM((ranks, per_chip), bf16),
            ],
        ),
        compiler_params=pltpu.CompilerParams(vmem_limit_bytes=vmem),
        cost_estimate=pl.CostEstimate(
            flops=6 * n_chips * rows * ranks * per_chip,
            bytes_accessed=3 * 2**20,
            transcendentals=2 * n_chips * rows * per_chip,
        ),
    )(core, own, other, packed)


def back_kernel(core_ref, own_ref, other_ref, new_ref, weight_ref, new_weight_ref, update_ref, dirs):
    @pl.when(pl.program_id(0) == 0)
    def _():
        n_chips, rows, width = other_ref.shape
        rows = rows // (n_chips + 1)
        core = core_ref[0]
        for ref, which in ((own_ref, core), (other_ref, 1 - core)):
            for block in range(n_chips):
                start = pl.multiple_of((2 * block + which) * rows, rows)
                for chip in range(n_chips):
                    dirs[pl.ds(start, rows), chip * width : (chip + 1) * width] = ref[
                        chip, block * rows : (block + 1) * rows, :
                    ]

    back = lax.dot_general(
        new_ref[...], dirs[...], (((1,), (1,)), ((), ())), preferred_element_type=f32
    )
    update_ref[...] = back.astype(bf16)
    new_weight_ref[...] = (weight_ref[...].astype(f32) - step_rate * back).astype(bf16)


def stepped(core, arrived, other, new_basis, weight):
    depth, ranks = new_basis.shape
    columns = weight.shape[1]
    steps = 4
    rows = depth // steps
    out = jax.ShapeDtypeStruct(weight.shape, bf16)
    block = pl.BlockSpec((rows, columns), lambda i, core: (i, 0))
    return pl.pallas_call(
        back_kernel,
        out_shape=(out, out),
        grid_spec=pltpu.PrefetchScalarGridSpec(
            num_scalar_prefetch=1,
            grid=(steps,),
            in_specs=[
                pl.BlockSpec(arrived.shape, lambda i, core: (0, 0, 0)),
                pl.BlockSpec(other.shape, lambda i, core: (0, 0, 0)),
                pl.BlockSpec((rows, ranks), lambda i, core: (i, 0)),
                block,
            ],
            out_specs=(block, block),
            scratch_shapes=[pltpu.VMEM((columns, ranks), bf16)],
        ),
        compiler_params=pltpu.CompilerParams(vmem_limit_bytes=24 * 2**20),
        cost_estimate=pl.CostEstimate(
            flops=2 * depth * columns * ranks, bytes_accessed=5 * 2**20, transcendentals=0
        ),
    )(core, arrived, other, new_basis, weight)


def shards(weight, gradient, old_basis, new_basis, first_moment, second_moment):
    ranks = new_basis.shape[1]
    n_chips = lax.axis_size("yh") * lax.axis_size("x")
    per_chip = ranks // n_chips
    columns = gradient.shape[1]
    own_columns = first_moment.shape[1]
    half = columns // 2
    core = lax.axis_index("c")

    residue = lax.axis_index("z") % 4
    pieces = trans_pieces(residue.reshape(1), old_basis, new_basis, n_chips)
    pieces, gradient = lax.optimization_barrier((pieces, gradient))
    pieces = lax.all_to_all(pieces, row, 0, 0, tiled=True)
    which = core.reshape(1)
    mine, low, high = grad_pieces(which, gradient, new_basis, n_chips, own_columns)
    low, high = swapped(low, "c"), swapped(high, "c")
    packed = packed_for(mine, low, high, first_moment.T, second_moment.T)
    packed, pieces = lax.optimization_barrier((packed, pieces))
    packed = exchanged(packed)

    trans = pieces.astype(f32).sum(0)
    quarters = [trans] + [turned(trans, "z", step) for step in (1, 2, 3)]
    trans = jnp.stack([chosen(quarters, (place - residue) % 4) for place in range(4)])
    other = swapped(trans, "c")
    lower = jnp.where(core == 0, trans, other)
    upper = jnp.where(core == 0, other, trans)
    arrived = exchanged(directions(jnp.zeros_like(which), lower, upper, packed))
    other = swapped(arrived, "c")
    new_weight, update = stepped(which, arrived, other, new_basis, weight)

    def joined(block):
        return block.transpose(1, 0, 2).reshape(own_columns, ranks).T

    second_new = arrived[:, half:].astype(f32)
    chip = lax.axis_index("yh") * lax.axis_size("x") + lax.axis_index("x")
    own = lax.dynamic_slice_in_dim(arrived, chip * own_columns, own_columns, 1).astype(f32)
    first_new = own * (jnp.sqrt(second_new) + epsilon)
    return new_weight, update, joined(first_new), joined(second_new)


def solution(mesh):
    fine = Mesh(mesh.devices.reshape(2, 4, 2, mesh.shape["col"] // 2, 2), names)
    split = P(row, col)
    moments = P(None, col + row)
    return jax.shard_map(
        shards,
        mesh=fine,
        in_specs=(split, split, P(row, None), P(row, None), moments, moments),
        out_specs=(split, split, moments, moments),
        check_vma=False,
    )
```

```python
import jax
import jax.numpy as jnp
from jax import lax
from jax.experimental import pallas as pl
from jax.experimental.pallas import tpu as pltpu
from jax.sharding import Mesh, PartitionSpec as P

beta_first = 0.9
beta_second = 0.95
epsilon = 1e-08
step_rate = 0.0025

names = ("yh", "x", "c", "z", "yl")
chips = ("yh", "x")
row = ("yh", "x", "c")
col = ("z", "yl")
vmem = 24 * 2**20
f32 = jnp.float32
bf16 = jnp.bfloat16


def swapped(value, axis):
    return lax.ppermute(value, axis, [(0, 1), (1, 0)])


def turned(value, axis, step):
    size = lax.axis_size(axis)

    def source(i):
        return i - i % 4 + (i + step) % 4

    return lax.ppermute(value, axis, [(source(i), i) for i in range(size)])


def chosen(values, which):
    out = values[0]
    for place in range(1, len(values)):
        out = jnp.where(which == place, values[place], out)
    return out


def exchanged(value):
    return lax.all_to_all(value, chips, 0, 0, tiled=True)


def transposed_product(left, right):
    return lax.dot_general(left, right, (((0,), (0,)), ((), ())), preferred_element_type=f32)


def whole(shape):
    return pl.BlockSpec(shape, lambda i, place: (0,) * len(shape))


def trans_kernel(place_ref, old_ref, new_ref, trans_ref):
    part = transposed_product(old_ref[...], new_ref[...])
    blocks, rows, per_chip = trans_ref.shape
    for block in range(blocks):
        chip, core = block // 2, block % 2
        piece = part[core * rows : (core + 1) * rows, chip * per_chip : (chip + 1) * per_chip]
        trans_ref[block] = piece.astype(trans_ref.dtype)


def trans_pieces(place, old_basis, new_basis, n_chips):
    depth, ranks = new_basis.shape
    quarter = ranks // 4
    steps = 1
    dims = (2 * n_chips, quarter // 2, ranks // n_chips)
    return pl.pallas_call(
        trans_kernel,
        out_shape=jax.ShapeDtypeStruct(dims, bf16),
        grid_spec=pltpu.PrefetchScalarGridSpec(
            num_scalar_prefetch=1,
            grid=(steps,),
            in_specs=[
                pl.BlockSpec((depth, quarter), lambda i, place: (0, place[0])),
                pl.BlockSpec((depth, ranks // steps), lambda i, place: (0, i)),
            ],
            out_specs=pl.BlockSpec((dims[0] // steps, *dims[1:]), lambda i, place: (i, 0, 0)),
        ),
        compiler_params=pltpu.CompilerParams(vmem_limit_bytes=60 * 2**20),
        cost_estimate=pl.CostEstimate(
            flops=2 * depth * quarter * ranks, bytes_accessed=2 * 2**20, transcendentals=0
        ),
    )(place, old_basis, new_basis)


def grad_kernel(core_ref, grad_ref, new_ref, mine_ref, low_ref, high_ref, total):
    total[...] = transposed_product(grad_ref[...], new_ref[...])
    n_chips, rows, ranks = mine_ref.shape
    per_chip = ranks // n_chips
    half = n_chips // 2
    core = core_ref[0]
    for block in range(n_chips):
        lanes = slice(block * per_chip, (block + 1) * per_chip)
        for own in (False, True):
            which = core if own else 1 - core
            start = pl.multiple_of((2 * block + which) * rows, rows)
            part = total[pl.ds(start, rows), :]
            for chip in range(n_chips):
                piece = part[:, chip * per_chip : (chip + 1) * per_chip]
                if own:
                    mine_ref[chip, :, lanes] = piece
                elif chip < half:
                    low_ref[chip, :, lanes] = piece.astype(bf16)
                else:
                    high_ref[chip - half, :, lanes] = piece.astype(bf16)


def grad_pieces(core, gradient, new_basis, n_chips, own_columns):
    depth, ranks = new_basis.shape
    columns = gradient.shape[1]
    dims = (n_chips, own_columns, ranks)
    part = (n_chips // 2, own_columns, ranks)
    return pl.pallas_call(
        grad_kernel,
        out_shape=(
            jax.ShapeDtypeStruct(dims, f32),
            jax.ShapeDtypeStruct(part, bf16),
            jax.ShapeDtypeStruct(part, bf16),
        ),
        grid_spec=pltpu.PrefetchScalarGridSpec(
            num_scalar_prefetch=1,
            grid=(1,),
            in_specs=[whole((depth, columns)), whole((depth, ranks))],
            out_specs=(whole(dims), whole(part), whole(part)),
            scratch_shapes=[pltpu.VMEM((columns, ranks), f32)],
        ),
        compiler_params=pltpu.CompilerParams(vmem_limit_bytes=vmem),
        cost_estimate=pl.CostEstimate(
            flops=2 * depth * columns * ranks, bytes_accessed=4 * 2**20, transcendentals=0
        ),
    )(core, gradient, new_basis)


def pack_kernel(mine_ref, low_ref, high_ref, first_ref, second_ref, out_ref):
    rows = first_ref.shape[0]
    n_chips = out_ref.shape[0]
    half = n_chips // 2
    both = jnp.concatenate([first_ref[...], second_ref[...]], 0).astype(bf16)
    for chip in range(n_chips):
        theirs = low_ref[chip] if chip < half else high_ref[chip - half]
        out_ref[chip, :rows] = (mine_ref[chip] + theirs.astype(f32)).astype(bf16)
        out_ref[chip, rows:] = both


def packed_for(mine, low, high, first_t, second_t):
    n_chips, rows, ranks = mine.shape
    return pl.pallas_call(
        pack_kernel,
        out_shape=jax.ShapeDtypeStruct((n_chips, 3 * rows, ranks), bf16),
        compiler_params=pltpu.CompilerParams(vmem_limit_bytes=vmem),
        cost_estimate=pl.CostEstimate(flops=1, bytes_accessed=1, transcendentals=0),
    )(mine, low, high, first_t, second_t)


def step_kernel(core_ref, own_ref, other_ref, packed_ref, out_ref, terms, squares):
    places, rows, per_chip = own_ref.shape
    core = core_ref[0]
    for ref, which in ((own_ref, core), (other_ref, 1 - core)):
        for place in range(places):
            start = pl.multiple_of((2 * place + which) * rows, rows)
            part = ref[place]
            high = part.astype(bf16)
            terms[pl.ds(start, rows), :per_chip] = high
            terms[pl.ds(start, rows), per_chip:] = (part - high.astype(f32)).astype(bf16)
            squares[pl.ds(start, rows), :] = (part * part).astype(bf16)
    n_chips, rows, ranks = packed_ref.shape
    rows = rows // 3
    half = n_chips * rows
    first_t = packed_ref[:, rows : 2 * rows, :].reshape(half, ranks)
    second_t = packed_ref[:, 2 * rows :, :].reshape(half, ranks)
    moved_first = jnp.dot(first_t, terms[...], preferred_element_type=f32)
    moved_first = moved_first[:, :per_chip] + moved_first[:, per_chip:]
    moved_second = jnp.dot(second_t, squares[...], preferred_element_type=f32)
    total = packed_ref[0, :rows, :].astype(f32)
    for chip in range(1, n_chips):
        total = total + packed_ref[chip, :rows, :].astype(f32)
    for block in range(n_chips):
        lines = slice(block * rows, (block + 1) * rows)
        projected = total[:, block * per_chip : (block + 1) * per_chip]
        first_new = beta_first * moved_first[lines] + (1.0 - beta_first) * projected
        second_new = beta_second * moved_second[lines] + (1.0 - beta_second) * projected * projected
        direction = (first_new / (jnp.sqrt(second_new) + epsilon)).astype(bf16)
        for chip in range(n_chips):
            out_ref[chip, lines, :] = direction
        out_ref[block, half:, :] = second_new.astype(bf16)


def directions(core, own, other, packed):
    n_chips, rows, ranks = packed.shape
    rows = rows // 3
    per_chip = own.shape[2]
    dims = (n_chips, (n_chips + 1) * rows, per_chip)
    return pl.pallas_call(
        step_kernel,
        out_shape=jax.ShapeDtypeStruct(dims, bf16),
        grid_spec=pltpu.PrefetchScalarGridSpec(
            num_scalar_prefetch=1,
            grid=(1,),
            in_specs=[whole(own.shape), whole(other.shape), whole(packed.shape)],
            out_specs=whole(dims),
            scratch_shapes=[
                pltpu.VMEM((ranks, 2 * per_chip), bf16),
                pltpu.VMEM((ranks, per_chip), bf16),
            ],
        ),
        compiler_params=pltpu.CompilerParams(vmem_limit_bytes=vmem),
        cost_estimate=pl.CostEstimate(
            flops=6 * n_chips * rows * ranks * per_chip,
            bytes_accessed=3 * 2**20,
            transcendentals=2 * n_chips * rows * per_chip,
        ),
    )(core, own, other, packed)


def back_kernel(core_ref, own_ref, other_ref, new_ref, weight_ref, new_weight_ref, update_ref, dirs):
    @pl.when(pl.program_id(0) == 0)
    def _():
        n_chips, rows, width = other_ref.shape
        rows = rows // (n_chips + 1)
        core = core_ref[0]
        for ref, which in ((own_ref, core), (other_ref, 1 - core)):
            for block in range(n_chips):
                start = pl.multiple_of((2 * block + which) * rows, rows)
                for chip in range(n_chips):
                    dirs[pl.ds(start, rows), chip * width : (chip + 1) * width] = ref[
                        chip, block * rows : (block + 1) * rows, :
                    ]

    back = lax.dot_general(
        new_ref[...], dirs[...], (((1,), (1,)), ((), ())), preferred_element_type=f32
    )
    update_ref[...] = back.astype(bf16)
    new_weight_ref[...] = (weight_ref[...].astype(f32) - step_rate * back).astype(bf16)


def stepped(core, arrived, other, new_basis, weight):
    depth, ranks = new_basis.shape
    columns = weight.shape[1]
    steps = 1
    rows = depth // steps
    out = jax.ShapeDtypeStruct(weight.shape, bf16)
    block = pl.BlockSpec((rows, columns), lambda i, core: (i, 0))
    return pl.pallas_call(
        back_kernel,
        out_shape=(out, out),
        grid_spec=pltpu.PrefetchScalarGridSpec(
            num_scalar_prefetch=1,
            grid=(steps,),
            in_specs=[
                pl.BlockSpec(arrived.shape, lambda i, core: (0, 0, 0)),
                pl.BlockSpec(other.shape, lambda i, core: (0, 0, 0)),
                pl.BlockSpec((rows, ranks), lambda i, core: (i, 0)),
                block,
            ],
            out_specs=(block, block),
            scratch_shapes=[pltpu.VMEM((columns, ranks), bf16)],
        ),
        compiler_params=pltpu.CompilerParams(vmem_limit_bytes=24 * 2**20),
        cost_estimate=pl.CostEstimate(
            flops=2 * depth * columns * ranks, bytes_accessed=5 * 2**20, transcendentals=0
        ),
    )(core, arrived, other, new_basis, weight)


def shards(weight, gradient, old_basis, new_basis, first_moment, second_moment):
    ranks = new_basis.shape[1]
    n_chips = lax.axis_size("yh") * lax.axis_size("x")
    per_chip = ranks // n_chips
    columns = gradient.shape[1]
    own_columns = first_moment.shape[1]
    half = columns // 2
    core = lax.axis_index("c")

    residue = lax.axis_index("z") % 4
    pieces = trans_pieces(residue.reshape(1), old_basis, new_basis, n_chips)
    pieces, gradient = lax.optimization_barrier((pieces, gradient))
    pieces = lax.all_to_all(pieces, row, 0, 0, tiled=True)
    which = core.reshape(1)
    mine, low, high = grad_pieces(which, gradient, new_basis, n_chips, own_columns)
    low, high = swapped(low, "c"), swapped(high, "c")
    packed = packed_for(mine, low, high, first_moment.T, second_moment.T)
    packed, pieces = lax.optimization_barrier((packed, pieces))
    packed = exchanged(packed)

    trans = pieces.astype(f32).sum(0)
    quarters = [trans] + [turned(trans, "z", step) for step in (1, 2, 3)]
    trans = jnp.stack([chosen(quarters, (place - residue) % 4) for place in range(4)])
    other = swapped(trans, "c")
    lower = jnp.where(core == 0, trans, other)
    upper = jnp.where(core == 0, other, trans)
    arrived = exchanged(directions(jnp.zeros_like(which), lower, upper, packed))
    other = swapped(arrived, "c")
    new_weight, update = stepped(which, arrived, other, new_basis, weight)

    def joined(block):
        return block.transpose(1, 0, 2).reshape(own_columns, ranks).T

    second_new = arrived[:, half:].astype(f32)
    chip = lax.axis_index("yh") * lax.axis_size("x") + lax.axis_index("x")
    own = lax.dynamic_slice_in_dim(arrived, chip * own_columns, own_columns, 1).astype(f32)
    first_new = own * (jnp.sqrt(second_new) + epsilon)
    return new_weight, update, joined(first_new), joined(second_new)


def solution(mesh):
    fine = Mesh(mesh.devices.reshape(2, 4, 2, mesh.shape["col"] // 2, 2), names)
    split = P(row, col)
    moments = P(None, col + row)
    return jax.shard_map(
        shards,
        mesh=fine,
        in_specs=(split, split, P(row, None), P(row, None), moments, moments),
        out_specs=(split, split, moments, moments),
        check_vma=False,
    )
```

```python
import jax
import jax.numpy as jnp
from jax import lax
from jax.experimental import pallas as pl
from jax.experimental.pallas import tpu as pltpu
from jax.sharding import Mesh, PartitionSpec as P

beta_first = 0.9
beta_second = 0.95
epsilon = 1e-08
step_rate = 0.0025

names = ("yh", "x", "c", "z", "yl")
chips = ("yh", "x")
row = ("yh", "x", "c")
col = ("z", "yl")
vmem = 24 * 2**20
f32 = jnp.float32
bf16 = jnp.bfloat16


def swapped(value, axis):
    return lax.ppermute(value, axis, [(0, 1), (1, 0)])


def turned(value, axis, step):
    size = lax.axis_size(axis)

    def source(i):
        return i - i % 4 + (i + step) % 4

    return lax.ppermute(value, axis, [(source(i), i) for i in range(size)])


def chosen(values, which):
    out = values[0]
    for place in range(1, len(values)):
        out = jnp.where(which == place, values[place], out)
    return out


def exchanged(value):
    return lax.all_to_all(value, chips, 0, 0, tiled=True)


def transposed_product(left, right):
    return lax.dot_general(left, right, (((0,), (0,)), ((), ())), preferred_element_type=f32)


def whole(shape):
    return pl.BlockSpec(shape, lambda i, place: (0,) * len(shape))


def trans_kernel(place_ref, old_ref, new_ref, trans_ref, old, new, trans, load, store):
    depth, quarter = old.shape
    blocks, rows, per_chip = trans.shape
    parts = store.shape[0]
    width = new.shape[1] // parts
    share = blocks // parts
    start = pl.multiple_of(place_ref[0] * quarter, quarter)
    loads = [pltpu.make_async_copy(old_ref.at[:, pl.ds(start, quarter)], old, load.at[parts])]
    for part in range(parts):
        lanes = pl.ds(part * width, width)
        loads.append(pltpu.make_async_copy(new_ref.at[:, lanes], new.at[:, lanes], load.at[part]))
    for copy in loads:
        copy.start()
    loads[0].wait()
    stores = []
    for part in range(parts):
        loads[part + 1].wait()
        total = transposed_product(old[...], new[:, part * width : (part + 1) * width])
        for block in range(share):
            chip, core = block // 2, block % 2
            piece = total[core * rows : (core + 1) * rows, chip * per_chip : (chip + 1) * per_chip]
            trans[part * share + block] = piece.astype(bf16)
        lines = pl.ds(part * share, share)
        stores.append(pltpu.make_async_copy(trans.at[lines], trans_ref.at[lines], store.at[part]))
        stores[-1].start()
    for copy in stores:
        copy.wait()


def trans_pieces(place, old_basis, new_basis, n_chips):
    depth, ranks = new_basis.shape
    quarter = ranks // 4
    parts = 2
    dims = (2 * n_chips, quarter // 2, ranks // n_chips)
    return pl.pallas_call(
        trans_kernel,
        out_shape=jax.ShapeDtypeStruct(dims, bf16),
        grid_spec=pltpu.PrefetchScalarGridSpec(
            num_scalar_prefetch=1,
            grid=(1,),
            in_specs=[pl.BlockSpec(memory_space=pl.ANY)] * 2,
            out_specs=pl.BlockSpec(memory_space=pl.ANY),
            scratch_shapes=[
                pltpu.VMEM((depth, quarter), bf16),
                pltpu.VMEM((depth, ranks), bf16),
                pltpu.VMEM(dims, bf16),
                pltpu.SemaphoreType.DMA((parts + 1,)),
                pltpu.SemaphoreType.DMA((parts,)),
            ],
        ),
        compiler_params=pltpu.CompilerParams(vmem_limit_bytes=60 * 2**20),
        cost_estimate=pl.CostEstimate(
            flops=2 * depth * quarter * ranks, bytes_accessed=2 * 2**20, transcendentals=0
        ),
    )(place, old_basis, new_basis)


def grad_kernel(core_ref, grad_ref, new_ref, mine_ref, low_ref, high_ref, total):
    total[...] = transposed_product(grad_ref[...], new_ref[...])
    n_chips, rows, ranks = mine_ref.shape
    per_chip = ranks // n_chips
    half = n_chips // 2
    core = core_ref[0]
    for block in range(n_chips):
        lanes = slice(block * per_chip, (block + 1) * per_chip)
        for own in (False, True):
            which = core if own else 1 - core
            start = pl.multiple_of((2 * block + which) * rows, rows)
            part = total[pl.ds(start, rows), :]
            for chip in range(n_chips):
                piece = part[:, chip * per_chip : (chip + 1) * per_chip]
                if own:
                    mine_ref[chip, :, lanes] = piece
                elif chip < half:
                    low_ref[chip, :, lanes] = piece.astype(bf16)
                else:
                    high_ref[chip - half, :, lanes] = piece.astype(bf16)


def grad_pieces(core, gradient, new_basis, n_chips, own_columns):
    depth, ranks = new_basis.shape
    columns = gradient.shape[1]
    dims = (n_chips, own_columns, ranks)
    part = (n_chips // 2, own_columns, ranks)
    return pl.pallas_call(
        grad_kernel,
        out_shape=(
            jax.ShapeDtypeStruct(dims, f32),
            jax.ShapeDtypeStruct(part, bf16),
            jax.ShapeDtypeStruct(part, bf16),
        ),
        grid_spec=pltpu.PrefetchScalarGridSpec(
            num_scalar_prefetch=1,
            grid=(1,),
            in_specs=[whole((depth, columns)), whole((depth, ranks))],
            out_specs=(whole(dims), whole(part), whole(part)),
            scratch_shapes=[pltpu.VMEM((columns, ranks), f32)],
        ),
        compiler_params=pltpu.CompilerParams(vmem_limit_bytes=vmem),
        cost_estimate=pl.CostEstimate(
            flops=2 * depth * columns * ranks, bytes_accessed=4 * 2**20, transcendentals=0
        ),
    )(core, gradient, new_basis)


def pack_kernel(mine_ref, low_ref, high_ref, first_ref, second_ref, out_ref):
    rows = first_ref.shape[0]
    n_chips = out_ref.shape[0]
    half = n_chips // 2
    both = jnp.concatenate([first_ref[...], second_ref[...]], 0).astype(bf16)
    for chip in range(n_chips):
        theirs = low_ref[chip] if chip < half else high_ref[chip - half]
        out_ref[chip, :rows] = (mine_ref[chip] + theirs.astype(f32)).astype(bf16)
        out_ref[chip, rows:] = both


def packed_for(mine, low, high, first_t, second_t):
    n_chips, rows, ranks = mine.shape
    return pl.pallas_call(
        pack_kernel,
        out_shape=jax.ShapeDtypeStruct((n_chips, 3 * rows, ranks), bf16),
        compiler_params=pltpu.CompilerParams(vmem_limit_bytes=vmem),
        cost_estimate=pl.CostEstimate(flops=1, bytes_accessed=1, transcendentals=0),
    )(mine, low, high, first_t, second_t)


def step_kernel(core_ref, own_ref, other_ref, packed_ref, out_ref, terms, squares):
    places, rows, per_chip = own_ref.shape
    core = core_ref[0]
    for ref, which in ((own_ref, core), (other_ref, 1 - core)):
        for place in range(places):
            start = pl.multiple_of((2 * place + which) * rows, rows)
            part = ref[place]
            high = part.astype(bf16)
            terms[pl.ds(start, rows), :per_chip] = high
            terms[pl.ds(start, rows), per_chip:] = (part - high.astype(f32)).astype(bf16)
            squares[pl.ds(start, rows), :] = (part * part).astype(bf16)
    n_chips, rows, ranks = packed_ref.shape
    rows = rows // 3
    half = n_chips * rows
    first_t = packed_ref[:, rows : 2 * rows, :].reshape(half, ranks)
    second_t = packed_ref[:, 2 * rows :, :].reshape(half, ranks)
    moved_first = jnp.dot(first_t, terms[...], preferred_element_type=f32)
    moved_first = moved_first[:, :per_chip] + moved_first[:, per_chip:]
    moved_second = jnp.dot(second_t, squares[...], preferred_element_type=f32)
    total = packed_ref[0, :rows, :].astype(f32)
    for chip in range(1, n_chips):
        total = total + packed_ref[chip, :rows, :].astype(f32)
    for block in range(n_chips):
        lines = slice(block * rows, (block + 1) * rows)
        projected = total[:, block * per_chip : (block + 1) * per_chip]
        first_new = beta_first * moved_first[lines] + (1.0 - beta_first) * projected
        second_new = beta_second * moved_second[lines] + (1.0 - beta_second) * projected * projected
        direction = (first_new / (jnp.sqrt(second_new) + epsilon)).astype(bf16)
        for chip in range(n_chips):
            out_ref[chip, lines, :] = direction
        out_ref[block, half:, :] = second_new.astype(bf16)


def directions(core, own, other, packed):
    n_chips, rows, ranks = packed.shape
    rows = rows // 3
    per_chip = own.shape[2]
    dims = (n_chips, (n_chips + 1) * rows, per_chip)
    return pl.pallas_call(
        step_kernel,
        out_shape=jax.ShapeDtypeStruct(dims, bf16),
        grid_spec=pltpu.PrefetchScalarGridSpec(
            num_scalar_prefetch=1,
            grid=(1,),
            in_specs=[whole(own.shape), whole(other.shape), whole(packed.shape)],
            out_specs=whole(dims),
            scratch_shapes=[
                pltpu.VMEM((ranks, 2 * per_chip), bf16),
                pltpu.VMEM((ranks, per_chip), bf16),
            ],
        ),
        compiler_params=pltpu.CompilerParams(vmem_limit_bytes=vmem),
        cost_estimate=pl.CostEstimate(
            flops=6 * n_chips * rows * ranks * per_chip,
            bytes_accessed=3 * 2**20,
            transcendentals=2 * n_chips * rows * per_chip,
        ),
    )(core, own, other, packed)


def back_kernel(core_ref, own_ref, other_ref, new_ref, weight_ref, new_weight_ref, update_ref, dirs):
    @pl.when(pl.program_id(0) == 0)
    def _():
        n_chips, rows, width = other_ref.shape
        rows = rows // (n_chips + 1)
        core = core_ref[0]
        for ref, which in ((own_ref, core), (other_ref, 1 - core)):
            for block in range(n_chips):
                start = pl.multiple_of((2 * block + which) * rows, rows)
                for chip in range(n_chips):
                    dirs[pl.ds(start, rows), chip * width : (chip + 1) * width] = ref[
                        chip, block * rows : (block + 1) * rows, :
                    ]

    back = lax.dot_general(
        new_ref[...], dirs[...], (((1,), (1,)), ((), ())), preferred_element_type=f32
    )
    update_ref[...] = back.astype(bf16)
    new_weight_ref[...] = (weight_ref[...].astype(f32) - step_rate * back).astype(bf16)


def stepped(core, arrived, other, new_basis, weight):
    depth, ranks = new_basis.shape
    columns = weight.shape[1]
    steps = 1
    rows = depth // steps
    out = jax.ShapeDtypeStruct(weight.shape, bf16)
    block = pl.BlockSpec((rows, columns), lambda i, core: (i, 0))
    return pl.pallas_call(
        back_kernel,
        out_shape=(out, out),
        grid_spec=pltpu.PrefetchScalarGridSpec(
            num_scalar_prefetch=1,
            grid=(steps,),
            in_specs=[
                pl.BlockSpec(arrived.shape, lambda i, core: (0, 0, 0)),
                pl.BlockSpec(other.shape, lambda i, core: (0, 0, 0)),
                pl.BlockSpec((rows, ranks), lambda i, core: (i, 0)),
                block,
            ],
            out_specs=(block, block),
            scratch_shapes=[pltpu.VMEM((columns, ranks), bf16)],
        ),
        compiler_params=pltpu.CompilerParams(vmem_limit_bytes=24 * 2**20),
        cost_estimate=pl.CostEstimate(
            flops=2 * depth * columns * ranks, bytes_accessed=5 * 2**20, transcendentals=0
        ),
    )(core, arrived, other, new_basis, weight)


def shards(weight, gradient, old_basis, new_basis, first_moment, second_moment):
    ranks = new_basis.shape[1]
    n_chips = lax.axis_size("yh") * lax.axis_size("x")
    per_chip = ranks // n_chips
    columns = gradient.shape[1]
    own_columns = first_moment.shape[1]
    half = columns // 2
    core = lax.axis_index("c")

    residue = lax.axis_index("z") % 4
    pieces = trans_pieces(residue.reshape(1), old_basis, new_basis, n_chips)
    pieces, gradient = lax.optimization_barrier((pieces, gradient))
    pieces = lax.all_to_all(pieces, row, 0, 0, tiled=True)
    which = core.reshape(1)
    mine, low, high = grad_pieces(which, gradient, new_basis, n_chips, own_columns)
    low, high = swapped(low, "c"), swapped(high, "c")
    packed = packed_for(mine, low, high, first_moment.T, second_moment.T)
    packed, pieces = lax.optimization_barrier((packed, pieces))
    packed = exchanged(packed)

    trans = pieces.astype(f32).sum(0)
    quarters = [trans] + [turned(trans, "z", step) for step in (1, 2, 3)]
    trans = jnp.stack([chosen(quarters, (place - residue) % 4) for place in range(4)])
    other = swapped(trans, "c")
    lower = jnp.where(core == 0, trans, other)
    upper = jnp.where(core == 0, other, trans)
    arrived = exchanged(directions(jnp.zeros_like(which), lower, upper, packed))
    other = swapped(arrived, "c")
    new_weight, update = stepped(which, arrived, other, new_basis, weight)

    def joined(block):
        return block.transpose(1, 0, 2).reshape(own_columns, ranks).T

    second_new = arrived[:, half:].astype(f32)
    chip = lax.axis_index("yh") * lax.axis_size("x") + lax.axis_index("x")
    own = lax.dynamic_slice_in_dim(arrived, chip * own_columns, own_columns, 1).astype(f32)
    first_new = own * (jnp.sqrt(second_new) + epsilon)
    return new_weight, update, joined(first_new), joined(second_new)


def solution(mesh):
    fine = Mesh(mesh.devices.reshape(2, 4, 2, mesh.shape["col"] // 2, 2), names)
    split = P(row, col)
    moments = P(None, col + row)
    return jax.shard_map(
        shards,
        mesh=fine,
        in_specs=(split, split, P(row, None), P(row, None), moments, moments),
        out_specs=(split, split, moments, moments),
        check_vma=False,
    )
```
